256 devices in a mesh: dp: 2 (over core), section: 8 (over z), et: 16 (over y, x).
Axes of the slice: x: 4, y: 4, z: 8, core: 2. Of those that a mesh axis runs over, the one named last changes fastest.
Arguments:
- acts: bfloat16 [16, 2, 1024, 4096], P(('dp', 'section'), None, 'et'), parts along dimension 0, may hold values from -6 to 6
- expert_ids: int32 [16, 2, 1024, 1], P(('dp', 'section'), None, 'et'), parts along dimension 0, may hold values from 0 to 3; in each aligned block of 64 rows (0 to 63, 64 to 127, ..., all dimensions but the last counted through in order) at most 24 rows name the same one
- gates: float32 [16, 2, 1024], P(('dp', 'section'), None, 'et'), parts along dimension 0, may hold values from 0.3 to 1
- norm_gain: float32 [16, 4096], P(('dp', 'section')), parts along dimension 0, may hold values from 0.5 to 1.5
- w_gate_up: bfloat16 [16, 16, 4096, 2, 384], P(('dp', 'section'), 'et'), parts along dimension 0, may hold values from -0.09375 to 0.09375
- w_down: bfloat16 [16, 16, 384, 4096], P(('dp', 'section'), 'et'), parts along dimension 0, may hold values from -0.15625 to 0.15625
Outputs:
- layer_out: bfloat16 [16, 2, 1024, 4096], P(('dp', 'section'), None, 'et'), parts along dimension 0
The draws below stay inside these ranges and needn't reach their ends.
There are 2 independent parts, one for each index of `dp`. The reference program is written for one: setup_inputs(seed, part) draws one part's arguments, and reference() takes and returns one part's arrays. A program takes and returns all parts, laid end to end along the dimension named above; each array names one. Nothing has to cross between parts.
Inputs may be any that keep to these rules, and one draw needn't show every extreme that they name: `expert_ids`: in each micro-batch, the 64 tokens of one device name one expert at most 24 times, and some device's tokens name some expert exactly 24 times.
All inputs are finite; a program needn't handle non-finite values.
Results may differ from the reference program's by a relative error of at most 0.0085.
Values may be sent and summed in bfloat16 or wider, within the bound.
No kernel may reach another device: no remote copies, remote signals or barrier semaphores. Data moves between devices by JAX's collectives and lax.ppermute only.
A program may use at most 128 MiB of HBM per device.

```python
import math
import jax
import jax.numpy as jnp
import numpy as np
from jax import lax

D = 4096
FF = 1536
QUARTERS = 4
MB = 2
TOK_DEV = 64
EXP_WIN = 4
FF_DEV = 384
CAP = 24
TOKENS_MB = 1024
N_SECTION = 8
N_ET = 16


def steps_of(rng, shape, pieces, low, top_value):
    def one(position, shards_of):
        heights = jax.random.uniform(jax.random.fold_in(jax.random.fold_in(rng, 6), position), (shards_of,), jnp.float32, low / len(pieces), top_value / len(pieces))
        return jnp.repeat(jnp.exp(heights), shape[position] // shards_of).reshape((-1,) + (1,) * (len(shape) - position - 1))

    factor_of = one(*pieces[0])
    for cut in pieces[1:]:
        factor_of = factor_of * one(*cut)
    return factor_of


def deal_out(key, own, number, rows, amount, top, limit, skew):
    ranking = jax.random.permutation(key, amount)
    packed, ordinary = load_shares(amount, rows * top, limit, skew, True), load_shares(amount, rows * top, limit, skew, False)
    places = jnp.arange(amount)

    def named(tallies, rotation):
        used = int((tallies > 0).sum())
        fixed = max(1, used // 4)
        moved = fixed + (places - fixed + rotation * (used - fixed)) % max(1, amount - fixed)
        return jnp.zeros((amount,), jnp.int32).at[ranking[jnp.where(places < fixed, places, moved)]].set(jnp.asarray(tallies, jnp.int32))

    tallies = jnp.where(number % 4 == 0, named(packed, number // 4), named(ordinary, number - number // 4 - 1))
    mixed = jax.random.permutation(jax.random.fold_in(own, 3), amount)
    giver, receiver = mixed[0:amount // 2 * 2:2], mixed[1:amount // 2 * 2:2]
    margin = jnp.minimum(tallies[giver] - 1, limit - tallies[receiver]) // 2
    margin = jnp.where((giver == ranking[0]) | (receiver == ranking[0]) | (tallies[receiver] == 0), 0, jnp.maximum(margin, 0))
    moved = jax.random.randint(jax.random.fold_in(own, 4), (amount // 2,), 0, 1 << 20) % (margin + 1)
    tallies = tallies.at[giver].add(-moved).at[receiver].add(moved)
    members = jnp.searchsorted(jnp.cumsum(tallies), jnp.arange(rows * top), side="right").astype(jnp.int32)
    listing = members.reshape(top, rows).T
    listing = listing[jax.random.permutation(jax.random.fold_in(own, 1), rows)]
    rotation = jax.random.randint(jax.random.fold_in(own, 2), (rows, 1), 0, top)
    return jnp.take_along_axis(listing, (jnp.arange(top)[None, :] + rotation) % top, axis=1)


def load_shares(count, total, most, lean, full):
    portions = [(1 << 20) // math.isqrt(rank ** lean) + 1 for rank in range(1, count + 1)]
    largest = most if full else min(most, max(-(-total // count), total * portions[0] // sum(portions)))
    least = 1 if total - largest >= count - 1 else 0
    holding, spare = [largest] + [least] * (count - 1), total - largest - least * (count - 1)
    while spare > 0:
        free = [i for i in range(1, count) if holding[i] < largest] or [i for i in range(1, count) if holding[i] < most]
        whole, budget = sum([portions[i] for i in free]), spare
        for i in free:
            addition = min(most - holding[i], max(1, budget * portions[i] // whole), spare)
            holding[i] = holding[i] + addition
            spare = spare - addition
    return np.array(holding)


def noise(key, extent, deviation, limit, cuts=(), kind=jnp.bfloat16):
    entries = jax.random.normal(key, extent, jnp.float32) * deviation
    if len(cuts) > 0:
        entries = steps_of(key, extent, cuts, -0.22, 0.18) * entries
    return jnp.clip(entries, min=-limit, max=limit).astype(kind)


def setup_inputs(seed: int = 0, part: int = 0) -> dict:
    streams_of = jax.random.split(jax.random.key(seed), 7)
    part_splits = jax.random.split(jax.random.fold_in(streams_of[6], part), 7)
    acts = noise(part_splits[0], (N_SECTION, MB, TOKENS_MB, D), 1.0, 6.0, ((0, 8), (2, 16)))
    expert_ids_keys = jax.random.split(jax.random.fold_in(part_splits[1], 1), N_SECTION * MB * TOKENS_MB // TOK_DEV)
    expert_ids_turns = jax.random.permutation(jax.random.fold_in(part_splits[1], 3), N_SECTION * MB * TOKENS_MB // TOK_DEV)
    expert_ids = jax.vmap(lambda own, number: deal_out(jax.random.fold_in(part_splits[1], 2), own, number, TOK_DEV, EXP_WIN, 1, CAP, 2))(expert_ids_keys, expert_ids_turns).reshape((N_SECTION, MB, TOKENS_MB, 1))
    gates = jnp.clip(0.3 + 0.7 * jax.random.uniform(part_splits[2], (N_SECTION, MB, TOKENS_MB), jnp.float32) ** steps_of(part_splits[2], (N_SECTION, MB, TOKENS_MB), ((0, 8), (2, 16)), -0.2, 0.2), 0.3, 1.0)
    norm_gain = jnp.clip(1.0 + 0.1 * jax.random.normal(part_splits[3], (N_SECTION, D), jnp.float32), 0.5, 1.5)
    w_gate_up = noise(part_splits[4], (N_SECTION, N_ET, D, 2, FF_DEV), D ** -0.5, 0.09375, ((0, 8), (1, 16)))
    w_down = noise(part_splits[5], (N_SECTION, N_ET, FF_DEV, D), FF ** -0.5, 0.15625, ((0, 8), (1, 16)))
    return {"acts": acts, "expert_ids": expert_ids, "gates": gates, "norm_gain": norm_gain, "w_gate_up": w_gate_up, "w_down": w_down}


def normalize(rows, gain):
    values = rows.astype(jnp.float32)
    scale = lax.rsqrt(lax.optimization_barrier(jnp.mean(values * values, axis=-1, keepdims=True)) + 1e-06)
    return (values * scale * gain).astype(jnp.bfloat16)

def slot_indices(chosen, expert):
    capacity = min(TOK_DEV, 3 * TOK_DEV // (2 * (N_ET // QUARTERS)))
    blocks = chosen.reshape(N_ET, TOK_DEV)
    matches = (blocks == expert).astype(jnp.int32)
    slot_rank = jnp.cumsum(matches, axis=1) - 1
    sources = jnp.arange(N_ET, dtype=jnp.int32)[:, None] * capacity
    slot_index = jnp.where(matches == 1, sources + slot_rank, N_ET * capacity)
    return (slot_index.reshape(-1).astype(jnp.int32), N_ET * capacity)

def segment_layer(inputs):
    arrive, ids, weights, gain, gate_up_w, down_w = inputs
    width = arrive.shape[-1]
    shard = FF // QUARTERS
    normed = normalize(arrive.reshape(-1, width), gain).reshape(arrive.shape)
    outputs = []
    for batch in range(arrive.shape[0]):
        chosen = ids[batch, :, 0]
        mixed = jnp.zeros((arrive.shape[1], width), jnp.float32)
        for expert in range(N_ET // QUARTERS):
            slot_index, slot_total = slot_indices(chosen, expert)
            buffer = jnp.zeros((slot_total + 1, width), jnp.float32).at[slot_index].set(normed[batch].astype(jnp.float32))[:slot_total]
            for quarter in range(QUARTERS):
                column = expert * QUARTERS + quarter
                stacked = gate_up_w[column].reshape(width, 2 * shard).astype(jnp.float32)
                both = jnp.dot(buffer, stacked, preferred_element_type=jnp.float32).reshape(-1, 2, shard)
                hidden = (jax.nn.silu(both[:, 0]) * both[:, 1]).astype(jnp.bfloat16).astype(jnp.float32)
                term = jnp.dot(hidden, down_w[column].astype(jnp.float32), preferred_element_type=jnp.float32)
                term = term.astype(jnp.bfloat16).astype(jnp.float32)
                padded = jnp.concatenate([term, jnp.zeros((1, width), jnp.float32)], axis=0)
                mixed = mixed + padded[slot_index]
        result = arrive[batch].astype(jnp.float32) + weights[batch][:, None] * mixed
        outputs.append(result.astype(jnp.bfloat16))
    return jnp.stack(outputs)

def reference(acts, expert_ids, gates, norm_gain, w_gate_up, w_down):
    arriving = jnp.roll(acts, 1, axis=0)
    return lax.map(segment_layer, (arriving, expert_ids, gates, norm_gain, w_gate_up, w_down))
```

```python
import jax
import jax.numpy as jnp
from jax import lax
from jax.sharding import PartitionSpec as P

SIDE = 4
CHUNKS = (("yx", 1024), ("yx", 1024), ("yx", 1024), ("yx", 1024))
BACK = (("xy", 1024), ("xy", 1024), ("xy", 1024), ("xy", 1024))
F32, BF16 = jnp.float32, jnp.bfloat16


def shift_z(v, by):
    n = lax.axis_size("section")
    return lax.ppermute(v, "section", [(i, (i + by) % n) for i in range(n)])


def shift_x(v, by):
    if by % SIDE == 0:
        return v
    return lax.ppermute(
        v, "et", [(i, i // SIDE * SIDE + (i + by) % SIDE) for i in range(SIDE * SIDE)]
    )


def shift_y(v, by):
    if by % SIDE == 0:
        return v
    n = SIDE * SIDE
    return lax.ppermute(v, "et", [(i, (i + SIDE * by) % n) for i in range(n)])


def gather_x(block):
    half = block.shape[0] // 2
    left, right = shift_x(block, 1), shift_x(block, -1)
    far = [shift_x(left[:half], 1), shift_x(right[half:], -1)]
    return [block, left, jnp.concatenate(far, 0), right]


def scatter_sum_x(parts):
    half = parts[0].shape[0] // 2
    add = lambda a, b: (a.astype(F32) + b.astype(F32)).astype(BF16)
    to_right = shift_x(parts[2][:half], 1)
    to_left = shift_x(parts[2][half:], -1)
    right = jnp.concatenate([add(parts[3][:half], to_right), parts[3][half:]], 0)
    left = jnp.concatenate([parts[1][:half], add(parts[1][half:], to_left)], 0)
    from_left, from_right = shift_x(right, 1), shift_x(left, -1)
    return parts[0].astype(F32) + from_left.astype(F32) + from_right.astype(F32)


def slot_map(ids, row, cap):
    batches, toks = ids.shape
    rel = (ids - row) % SIDE
    same = (rel[:, :, None] == rel[:, None, :]) & (
        jnp.arange(toks)[:, None] > jnp.arange(toks)[None, :]
    )
    rank = jnp.sum(same.astype(jnp.int32), axis=2)
    target = rel * (batches * cap) + jnp.arange(batches)[:, None] * cap + rank
    slots = SIDE * batches * cap
    return (jnp.arange(slots)[:, None] == target.reshape(1, -1)).astype(BF16)


def place(onehot, rows):
    return jnp.dot(onehot, rows, preferred_element_type=F32)


def per_device(acts, expert_ids, gates, norm_gain, w_gate_up, w_down):
    _, batches, toks, width = acts.shape
    cap = min(toks, 3 * toks // (2 * SIDE))
    per = batches * cap
    row = lax.axis_index("et") // SIDE
    hidden_dev = w_down.shape[2]
    own = acts[0].reshape(batches * toks, width)
    starts, pos = [], 0
    for _, c in CHUNKS:
        starts.append(pos)
        pos += c
    arriving = [shift_z(own[:, s : s + c], 1) for s, (_, c) in zip(starts, CHUNKS)]

    ids = expert_ids[0, :, :, 0]
    need_row = any(m == "xy" for m, _ in CHUNKS) or any(m == "yx" for m, _ in BACK)
    maps = [slot_map(ids, row, cap)]
    if need_row:
        wire = ids.astype(F32)
        maps += [
            slot_map(shift_x(wire, j).astype(jnp.int32), row, cap) for j in range(1, SIDE)
        ]

    gate_up = (
        w_gate_up[0, 0].reshape(width, 2 * hidden_dev).astype(F32) * norm_gain[0][:, None]
    ).astype(BF16)

    total, squares = 0.0, 0.0
    for s, (mode, c), arr in zip(starts, CHUNKS, arriving):
        if mode == "yx":
            slots = place(maps[0], arr).astype(BF16).reshape(SIDE, per, c)
            got = jnp.concatenate([shift_y(slots[k], k) for k in range(SIDE)], 0)
            rows = jnp.concatenate(gather_x(got), 0)
        else:
            slots = [
                place(m, t).astype(BF16).reshape(SIDE, per, c)
                for m, t in zip(maps, gather_x(arr))
            ]
            got = [
                shift_y(jnp.stack([slots[j][k] for j in range(SIDE)]), k) for k in range(SIDE)
            ]
            rows = jnp.stack(got, 1).reshape(SIDE * SIDE * per, c)
        total = total + jnp.dot(rows, gate_up[s : s + c], preferred_element_type=F32)
        squares = squares + jnp.sum(jnp.square(rows.astype(F32)), axis=1, keepdims=True)
    both = total * lax.rsqrt(squares * (1.0 / width) + 1e-06)
    hidden = (jax.nn.silu(both[:, :hidden_dev]) * both[:, hidden_dev:]).astype(BF16)

    whole = jnp.concatenate(arriving, axis=1)
    down = w_down[0, 0]
    gate = gates[0].reshape(-1, 1)
    outs, s = [], 0
    for mode, c in BACK:
        part = jnp.dot(hidden, down[:, s : s + c], preferred_element_type=F32).astype(BF16)
        part = part.reshape(SIDE, SIDE, per, c)
        if mode == "xy":
            mine = scatter_sum_x([part[j].reshape(SIDE * per, c) for j in range(SIDE)])
            mine = mine.astype(BF16).reshape(SIDE, per, c)
            back = jnp.concatenate([shift_y(mine[k], -k) for k in range(SIDE)], 0)
            sums = place(maps[0].T, back)
        else:
            back = [shift_y(part[:, k], -k) for k in range(SIDE)]
            sums = scatter_sum_x(
                [
                    place(maps[j].T, jnp.concatenate([b[j] for b in back], 0)).astype(BF16)
                    for j in range(SIDE)
                ]
            )
        outs.append((whole[:, s : s + c].astype(F32) + gate * sums).astype(BF16))
        s += c
    return jnp.concatenate(outs, 1).reshape(1, batches, toks, width)


def solution(mesh):
    in_specs = (
        P(("dp", "section"), None, "et", None),
        P(("dp", "section"), None, "et", None),
        P(("dp", "section"), None, "et"),
        P(("dp", "section"), None),
        P(("dp", "section"), "et", None, None, None),
        P(("dp", "section"), "et", None, None),
    )
    out_specs = P(("dp", "section"), None, "et", None)
    return jax.shard_map(
        per_device, mesh=mesh, in_specs=in_specs, out_specs=out_specs, check_vma=False
    )
```

```python
import jax
import jax.numpy as jnp
from jax import lax
from jax.sharding import PartitionSpec as P

SIDE = 4
F32, BF16 = jnp.float32, jnp.bfloat16


def shift_z(v, by):
    n = lax.axis_size("section")
    return lax.ppermute(v, "section", [(i, (i + by) % n) for i in range(n)])


def shift_x(v, by):
    pairs = [(i, i // SIDE * SIDE + (i + by) % SIDE) for i in range(SIDE * SIDE)]
    return lax.ppermute(v, "et", pairs)


def shift_y(v, by):
    n = SIDE * SIDE
    return lax.ppermute(v, "et", [(i, (i + SIDE * by) % n) for i in range(n)])


def shift_zy(v, by):
    n, m = lax.axis_size("section"), SIDE * SIDE
    pairs = [
        (z * m + i, (z + 1) % n * m + (i + SIDE * by) % m) for z in range(n) for i in range(m)
    ]
    return lax.ppermute(v, ("section", "et"), pairs)


def gather_x(block):
    half = block.shape[0] // 2
    left, right = shift_x(block, 1), shift_x(block, -1)
    far = [shift_x(left[:half], 1), shift_x(right[half:], -1)]
    return jnp.concatenate([block, left, *far, right], 0)


def scatter_sum_x(parts):
    half = parts[0].shape[0] // 2
    add = lambda a, b: (a.astype(F32) + b.astype(F32)).astype(BF16)
    to_right = shift_x(parts[2][:half], 1)
    to_left = shift_x(parts[2][half:], -1)
    right = jnp.concatenate([add(parts[3][:half], to_right), parts[3][half:]], 0)
    left = jnp.concatenate([parts[1][:half], add(parts[1][half:], to_left)], 0)
    from_left, from_right = shift_x(right, 1), shift_x(left, -1)
    return parts[0].astype(F32) + from_left.astype(F32) + from_right.astype(F32)


def slot_map(ids, row, cap):
    toks = ids.shape[0]
    same = (ids[:, None] == ids[None, :]) & (
        jnp.arange(toks)[:, None] > jnp.arange(toks)[None, :]
    )
    rank = jnp.sum(same.astype(jnp.int32), axis=1)
    target = (ids - row) % SIDE * cap + rank
    slots = jnp.arange(SIDE * cap)[:, None] == target[None, :]
    return slots.astype(BF16).reshape(SIDE, cap, toks)


def normalize(rows, gain):
    values = rows.astype(F32)
    scale = lax.rsqrt(jnp.mean(values * values, axis=-1, keepdims=True) + 1e-06)
    return (values * scale * gain).astype(BF16)


def per_device(acts, expert_ids, gates, norm_gain, w_gate_up, w_down):
    _, batches, toks, width = acts.shape
    cap = min(toks, 3 * toks // (2 * SIDE))
    row = lax.axis_index("et") // SIDE
    ids = expert_ids[0, :, :, 0]
    asked = shift_z(jnp.concatenate([ids.reshape(-1).astype(F32), norm_gain[0]]), -1)
    next_ids = asked[: batches * toks].astype(jnp.int32).reshape(batches, toks)
    next_gain = asked[batches * toks :]

    mine = []
    for b in range(batches):
        normed = normalize(acts[0, b], next_gain)
        to_slots = slot_map(next_ids[b], row, cap)
        mine.append(
            jnp.concatenate(
                [
                    shift_zy(
                        jnp.dot(to_slots[k], normed, preferred_element_type=F32).astype(BF16), k
                    )
                    for k in range(SIDE)
                ],
                0,
            )
        )

    hidden = []
    for b in range(batches):
        rows = gather_x(mine[b])
        both = jnp.einsum("rd,dkf->rkf", rows, w_gate_up[0, 0], preferred_element_type=F32)
        hidden.append((jax.nn.silu(both[:, 0]) * both[:, 1]).astype(BF16))

    held = acts[0] * (1.0 + 0.0 * mine[-1][0, 0])
    arriving = shift_z(held, 1)
    outs = []
    for b in range(batches):
        part = jnp.dot(hidden[b], w_down[0, 0], preferred_element_type=F32).astype(BF16)
        part = part.reshape(SIDE, SIDE * cap, width)
        summed = scatter_sum_x([part[j] for j in range(SIDE)]).astype(BF16)
        summed = summed.reshape(SIDE, cap, width)
        back = [summed[0]] + [shift_y(summed[k], -k) for k in range(1, SIDE)]
        from_slots = slot_map(ids[b], row, cap).reshape(SIDE * cap, toks).T
        sums = jnp.dot(from_slots, jnp.concatenate(back, 0), preferred_element_type=F32)
        outs.append((arriving[b].astype(F32) + gates[0, b][:, None] * sums).astype(BF16))
    return jnp.stack(outs)[None]


def solution(mesh):
    in_specs = (
        P(("dp", "section"), None, "et", None),
        P(("dp", "section"), None, "et", None),
        P(("dp", "section"), None, "et"),
        P(("dp", "section"), None),
        P(("dp", "section"), "et", None, None, None),
        P(("dp", "section"), "et", None, None),
    )
    out_specs = P(("dp", "section"), None, "et", None)
    return jax.shard_map(
        per_device, mesh=mesh, in_specs=in_specs, out_specs=out_specs, check_vma=False
    )
```

```python
import jax
import jax.numpy as jnp
from jax import lax
from jax.experimental import pallas as pl
from jax.experimental.pallas import tpu as pltpu
from jax.sharding import PartitionSpec as P

SIDE = 4
THERE = ((4096,), (4096,))
BACK = ((4096,), (4096,))
F32, BF16 = jnp.float32, jnp.bfloat16


def shift_z(v, by):
    n = lax.axis_size("section")
    return lax.ppermute(v, "section", [(i, (i + by) % n) for i in range(n)])


def shift_x(v, by):
    pairs = [(i, i // SIDE * SIDE + (i + by) % SIDE) for i in range(SIDE * SIDE)]
    return lax.ppermute(v, "et", pairs)


def shift_y(v, by):
    n = SIDE * SIDE
    return lax.ppermute(v, "et", [(i, (i + SIDE * by) % n) for i in range(n)])


def shift_zy(v, by):
    n, m = lax.axis_size("section"), SIDE * SIDE
    pairs = [
        (z * m + i, (z + 1) % n * m + (i + SIDE * by) % m) for z in range(n) for i in range(m)
    ]
    return lax.ppermute(v, ("section", "et"), pairs)


def gather_x(block):
    half = block.shape[0] // 2
    left, right = shift_x(block, 1), shift_x(block, -1)
    far = [shift_x(left[:half], 1), shift_x(right[half:], -1)]
    return [block, left, *far, right]


def tied(rows, *after):
    zero = sum(v[0, 0].astype(F32) for v in after) * 0.0
    return rows * (1.0 + zero).astype(rows.dtype)


def scatter_sum_x(parts):
    half = parts[0].shape[0] // 2
    add = lambda a, b: (a.astype(F32) + b.astype(F32)).astype(BF16)
    to_right = shift_x(parts[2][:half], 1)
    to_left = shift_x(parts[2][half:], -1)
    right = jnp.concatenate([add(parts[3][:half], to_right), parts[3][half:]], 0)
    left = jnp.concatenate([parts[1][:half], add(parts[1][half:], to_left)], 0)
    from_left, from_right = shift_x(right, 1), shift_x(left, -1)
    return parts[0].astype(F32) + from_left.astype(F32) + from_right.astype(F32)


def slot_map(ids, row, cap):
    toks = ids.shape[0]
    same = (ids[:, None] == ids[None, :]) & (
        jnp.arange(toks)[:, None] > jnp.arange(toks)[None, :]
    )
    rank = jnp.sum(same.astype(jnp.int32), axis=1)
    target = (ids - row) % SIDE * cap + rank
    return (jnp.arange(SIDE * cap)[:, None] == target[None, :]).astype(BF16)


def spans(sizes):
    return [(sum(sizes[:i]), c) for i, c in enumerate(sizes)]


def pack(acts, batch, gain, onehot, sizes, after):
    cap = onehot.shape[0] // SIDE
    toks, width = acts.shape[2:]

    def kernel(a, g, s, *rest):
        outs = rest[len(after) :]
        values = a[0, 0].astype(F32)
        scale = lax.rsqrt(jnp.mean(values * values, axis=-1, keepdims=True) + 1e-06)
        for n, (start, c) in enumerate(spans(sizes)):
            cols = slice(start, start + c)
            normed = (values[:, cols] * scale * g[:, cols]).astype(BF16)
            slots = jnp.dot(s[...], normed, preferred_element_type=F32)
            for k in range(SIDE):
                outs[SIDE * n + k][...] = slots[k * cap : (k + 1) * cap].astype(BF16)

    def full(shape):
        return pl.BlockSpec(shape, lambda i: (0,) * len(shape))

    outs = pl.pallas_call(
        kernel,
        grid=(1,),
        out_shape=[jax.ShapeDtypeStruct((cap, c), BF16) for c in sizes for _ in range(SIDE)],
        in_specs=[
            pl.BlockSpec((1, 1, toks, width), lambda i: (0, batch, 0, 0)),
            full((1, width)),
            full(onehot.shape),
            *[full(v.shape) for v in after],
        ],
        out_specs=[full((cap, c)) for c in sizes for _ in range(SIDE)],
        compiler_params=pltpu.CompilerParams(vmem_limit_bytes=12 << 20),
        name="pack",
    )(acts, gain, onehot, *after)
    return [outs[SIDE * n : SIDE * (n + 1)] for n in range(len(sizes))]


def per_device(acts, expert_ids, gates, norm_gain, w_gate_up, w_down):
    _, batches, toks, width = acts.shape
    cap = min(toks, 3 * toks // (2 * SIDE))
    row = lax.axis_index("et") // SIDE
    ids = expert_ids[0, :, :, 0]
    asked = shift_z(jnp.concatenate([ids.reshape(-1).astype(F32), norm_gain[0]]), -1)
    next_ids = asked[: batches * toks].astype(jnp.int32).reshape(batches, toks)
    next_gain = asked[batches * toks :].reshape(1, width)

    pieces = []
    for b in range(batches):
        onehot = slot_map(next_ids[b], row, cap)
        for p in pack(acts, b, next_gain, onehot, THERE[b], []):
            pieces.append((b, [shift_zy(p[k], k) for k in range(SIDE)]))

    gathered = [[] for _ in range(batches)]
    for b, piece in pieces:
        mine = jnp.concatenate(piece, 0)
        blocks = gather_x(mine)
        gathered[b].append(jnp.concatenate(blocks, 0))

    hidden = []
    for b in range(batches):
        rows = jnp.concatenate(gathered[b], 1)
        both = jnp.einsum("rd,dkf->rkf", rows, w_gate_up[0, 0], preferred_element_type=F32)
        hidden.append((jax.nn.silu(both[:, 0]) * both[:, 1]).astype(BF16))

    arriving = shift_z(tied(acts[0], *[p[:1, :1] for p in pieces[-1][1]]), 1)
    outs = []
    for b in range(batches):
        from_slots = slot_map(ids[b], row, cap).T
        done = []
        for s, c in spans(BACK[b]):
            part = jnp.dot(hidden[b], w_down[0, 0, :, s : s + c], preferred_element_type=F32)
            part = part.astype(BF16).reshape(SIDE, SIDE * cap, c)
            summed = scatter_sum_x([part[j] for j in range(SIDE)]).astype(BF16)
            summed = summed.reshape(SIDE, cap, c)
            back = [summed[0]] + [shift_y(summed[k], -k) for k in range(1, SIDE)]
            sums = jnp.dot(from_slots, jnp.concatenate(back, 0), preferred_element_type=F32)
            own = arriving[b, :, s : s + c].astype(F32)
            done.append((own + gates[0, b][:, None] * sums).astype(BF16))
        outs.append(jnp.concatenate(done, 1))
    return jnp.stack(outs)[None]


def solution(mesh):
    in_specs = (
        P(("dp", "section"), None, "et", None),
        P(("dp", "section"), None, "et", None),
        P(("dp", "section"), None, "et"),
        P(("dp", "section"), None),
        P(("dp", "section"), "et", None, None, None),
        P(("dp", "section"), "et", None, None),
    )
    out_specs = P(("dp", "section"), None, "et", None)
    return jax.shard_map(
        per_device, mesh=mesh, in_specs=in_specs, out_specs=out_specs, check_vma=False
    )
```

```python
import jax
import jax.numpy as jnp
from jax import lax
from jax.experimental import pallas as pl
from jax.experimental.pallas import tpu as pltpu
from jax.sharding import PartitionSpec as P

SIDE = 4
F32, BF16 = jnp.float32, jnp.bfloat16


def shift_z(v, by):
    n = lax.axis_size("section")
    return lax.ppermute(v, "section", [(i, (i + by) % n) for i in range(n)])


def shift_x(v, by):
    pairs = [(i, i // SIDE * SIDE + (i + by) % SIDE) for i in range(SIDE * SIDE)]
    return lax.ppermute(v, "et", pairs)


def shift_y(v, by):
    n = SIDE * SIDE
    return lax.ppermute(v, "et", [(i, (i + SIDE * by) % n) for i in range(n)])


def gather_x(block):
    half = block.shape[0] // 2
    left, right = shift_x(block, 1), shift_x(block, -1)
    far = [shift_x(left[:half], 1), shift_x(right[half:], -1)]
    return [block, left, *far, right]


def scatter_sum_x(parts):
    half = parts[0].shape[0] // 2
    add = lambda a, b: (a.astype(F32) + b.astype(F32)).astype(BF16)
    to_right = shift_x(parts[2][:half], 1)
    to_left = shift_x(parts[2][half:], -1)
    right = jnp.concatenate([add(parts[3][:half], to_right), parts[3][half:]], 0)
    left = jnp.concatenate([parts[1][:half], add(parts[1][half:], to_left)], 0)
    from_left, from_right = shift_x(right, 1), shift_x(left, -1)
    return parts[0].astype(F32) + from_left.astype(F32) + from_right.astype(F32)


def slot_map(ids, row, cap):
    toks = ids.shape[0]
    same = (ids[:, None] == ids[None, :]) & (
        jnp.arange(toks)[:, None] > jnp.arange(toks)[None, :]
    )
    rank = jnp.sum(same.astype(jnp.int32), axis=1)
    target = (ids - row) % SIDE * cap + rank
    return (jnp.arange(SIDE * cap)[:, None] == target[None, :]).astype(BF16)


def whole(shape):
    return pl.BlockSpec(shape, lambda i: (0,) * len(shape))


def batch_of(shape, batch):
    return pl.BlockSpec((1, *shape[1:]), lambda i: (batch,) + (0,) * (len(shape) - 1))


def pack(rows, batch, gain, routing, row, cap, after):
    toks, width = rows.shape[1:]

    def kernel(base, a, g, r, *rest):
        outs = rest[len(after) :]
        i, j = (lax.broadcasted_iota(jnp.int32, (toks, toks), d) for d in range(2))
        across = jnp.broadcast_to(r[...], (toks, toks))
        down = jnp.sum(jnp.where(i == j, across, 0.0), 1, keepdims=True)
        earlier = jnp.where((across == down) & (j < i), 1.0, 0.0)
        rank = jnp.sum(earlier, 1, keepdims=True).astype(jnp.int32)
        target = lax.rem(down.astype(jnp.int32) - base[0] + SIDE, SIDE) * cap + rank
        slot = lax.broadcasted_iota(jnp.int32, (toks, SIDE * cap), 1)
        onehot = jnp.where(slot == target, 1.0, 0.0).astype(BF16)
        values = a[0].astype(F32)
        scale = lax.rsqrt(jnp.mean(values * values, axis=-1, keepdims=True) + 1e-06)
        normed = (values * scale * g[...]).astype(BF16)
        slots = lax.dot_general(
            onehot, normed, (((0,), (0,)), ((), ())), preferred_element_type=F32
        )
        for k in range(SIDE):
            outs[k][...] = slots[k * cap : (k + 1) * cap].astype(BF16)

    return pl.pallas_call(
        kernel,
        grid=(1,),
        out_shape=[jax.ShapeDtypeStruct((cap, width), BF16)] * SIDE,
        in_specs=[
            pl.BlockSpec(memory_space=pltpu.SMEM),
            batch_of(rows.shape, batch),
            whole(gain.shape),
            whole(routing.shape),
            *[pl.BlockSpec((16, 128), lambda i: (0, 0)) for _ in after],
        ],
        out_specs=[whole((cap, width))] * SIDE,
        compiler_params=pltpu.CompilerParams(vmem_limit_bytes=12 << 20),
        name="pack",
    )(row, rows, gain, routing, *after)


def finish(raw, batch, gate, onehot, back, earlier):
    toks, width = raw.shape[1:]

    def kernel(r, g, s, *rest):
        out = rest[-1]
        i, j = (lax.broadcasted_iota(jnp.int32, (toks, toks), d) for d in range(2))
        scale = jnp.sum(jnp.where(i == j, g[batch : batch + 1], 0.0), 1, keepdims=True)
        if earlier:
            out[:batch] = rest[SIDE][...]
        sums = sum(
            lax.dot_general(
                s[k], rest[k][...], (((0,), (0,)), ((), ())), preferred_element_type=F32
            )
            for k in range(SIDE)
        )
        out[batch] = (r[0].astype(F32) + scale * sums).astype(BF16)

    shape = (batch + 1, toks, width)
    return pl.pallas_call(
        kernel,
        grid=(1,),
        out_shape=jax.ShapeDtypeStruct(shape, BF16),
        in_specs=[
            batch_of(raw.shape, 0),
            *[whole(v.shape) for v in (gate, onehot, *back, *earlier)],
        ],
        out_specs=whole(shape),
        compiler_params=pltpu.CompilerParams(vmem_limit_bytes=16 << 20),
        name="finish",
    )(raw, gate, onehot, *back, *earlier)


def per_device(acts, expert_ids, gates, norm_gain, w_gate_up, w_down):
    _, batches, toks, width = acts.shape
    cap = min(toks, 3 * toks // (2 * SIDE))
    row = lax.axis_index("et") // SIDE
    ids = expert_ids[0, :, :, 0]
    arriving = [shift_z(acts[0, b : b + 1], 1) for b in range(batches)]
    mine = []
    for b in range(batches):
        routing = ids[b : b + 1].astype(F32)
        packed = pack(arriving[b], 0, norm_gain, routing, row[None], cap, mine)
        landed = [packed[0]] + [shift_y(packed[k], k) for k in range(1, SIDE)]
        mine.append(jnp.concatenate(landed, 0))

    hidden = []
    for b in range(batches):
        rows = jnp.concatenate(gather_x(mine[b]), 0)
        both = jnp.einsum("rd,dkf->rkf", rows, w_gate_up[0, 0], preferred_element_type=F32)
        hidden.append((jax.nn.silu(both[:, 0]) * both[:, 1]).astype(BF16))

    out = []
    for b in range(batches):
        part = jnp.dot(hidden[b], w_down[0, 0], preferred_element_type=F32).astype(BF16)
        part = part.reshape(SIDE, SIDE * cap, width)
        summed = scatter_sum_x([part[j] for j in range(SIDE)]).astype(BF16)
        summed = summed.reshape(SIDE, cap, width)
        back = [summed[0]] + [shift_y(summed[k], -k) for k in range(1, SIDE)]
        onehot = slot_map(ids[b], row, cap).reshape(SIDE, cap, toks)
        out = [finish(arriving[b], b, gates[0], onehot, back, out)]
    return out[0][None]


def solution(mesh):
    in_specs = (
        P(("dp", "section"), None, "et", None),
        P(("dp", "section"), None, "et", None),
        P(("dp", "section"), None, "et"),
        P(("dp", "section"), None),
        P(("dp", "section"), "et", None, None, None),
        P(("dp", "section"), "et", None, None),
    )
    out_specs = P(("dp", "section"), None, "et", None)
    return jax.shard_map(
        per_device, mesh=mesh, in_specs=in_specs, out_specs=out_specs, check_vma=False
    )
```

```python
import jax
import jax.numpy as jnp
from jax import lax
from jax.experimental import pallas as pl
from jax.experimental.pallas import tpu as pltpu
from jax.sharding import PartitionSpec as P

SIDE = 4
BACK = ((4096,), (4096,))
F32, BF16 = jnp.float32, jnp.bfloat16


def shift_z(v, by):
    n = lax.axis_size("section")
    return lax.ppermute(v, "section", [(i, (i + by) % n) for i in range(n)])


def shift_x(v, by):
    pairs = [(i, i // SIDE * SIDE + (i + by) % SIDE) for i in range(SIDE * SIDE)]
    return lax.ppermute(v, "et", pairs)


def shift_y(v, by):
    n = SIDE * SIDE
    return lax.ppermute(v, "et", [(i, (i + SIDE * by) % n) for i in range(n)])


def gather_x(block):
    half = block.shape[0] // 2
    left, right = shift_x(block, 1), shift_x(block, -1)
    far = [shift_x(left[:half], 1), shift_x(right[half:], -1)]
    return [block, left, *far, right]


def scatter_sum_x(parts, sizes):
    half = parts[0].shape[0] // 2
    add = lambda a, b: (a.astype(F32) + b.astype(F32)).astype(BF16)
    to_right = shift_x(parts[2][:half], 1)
    to_left = shift_x(parts[2][half:], -1)
    sums, start = [], 0
    for c in sizes:
        cols = slice(start, start + c)
        start += c
        right = jnp.concatenate(
            [add(parts[3][:half, cols], to_right[:, cols]), parts[3][half:, cols]], 0
        )
        left = jnp.concatenate(
            [parts[1][:half, cols], add(parts[1][half:, cols], to_left[:, cols])], 0
        )
        from_left, from_right = shift_x(right, 1), shift_x(left, -1)
        total = parts[0][:, cols].astype(F32) + from_left.astype(F32) + from_right.astype(F32)
        sums.append(total.astype(BF16))
    return sums


def slot_map(ids, row, cap):
    toks = ids.shape[0]
    same = (ids[:, None] == ids[None, :]) & (
        jnp.arange(toks)[:, None] > jnp.arange(toks)[None, :]
    )
    rank = jnp.sum(same.astype(jnp.int32), axis=1)
    target = (ids - row) % SIDE * cap + rank
    return (jnp.arange(SIDE * cap)[:, None] == target[None, :]).astype(BF16)


def whole(shape):
    return pl.BlockSpec(shape, lambda i: (0,) * len(shape))


def batch_of(shape, batch):
    return pl.BlockSpec((1, *shape[1:]), lambda i: (batch,) + (0,) * (len(shape) - 1))


def pack(rows, batch, gain, routing, row, cap, after):
    toks, width = rows.shape[1:]

    def kernel(base, a, g, r, *rest):
        outs = rest[len(after) :]
        i, j = (lax.broadcasted_iota(jnp.int32, (toks, toks), d) for d in range(2))
        across = jnp.broadcast_to(r[...], (toks, toks))
        down = jnp.sum(jnp.where(i == j, across, 0.0), 1, keepdims=True)
        earlier = jnp.where((across == down) & (j < i), 1.0, 0.0)
        rank = jnp.sum(earlier, 1, keepdims=True).astype(jnp.int32)
        target = lax.rem(down.astype(jnp.int32) - base[0] + SIDE, SIDE) * cap + rank
        slot = lax.broadcasted_iota(jnp.int32, (toks, SIDE * cap), 1)
        onehot = jnp.where(slot == target, 1.0, 0.0).astype(BF16)
        values = a[0].astype(F32)
        scale = lax.rsqrt(jnp.mean(values * values, axis=-1, keepdims=True) + 1e-06)
        normed = (values * scale * g[...]).astype(BF16)
        slots = lax.dot_general(
            onehot, normed, (((0,), (0,)), ((), ())), preferred_element_type=F32
        )
        for k in range(SIDE):
            outs[k][...] = slots[k * cap : (k + 1) * cap].astype(BF16)

    return pl.pallas_call(
        kernel,
        grid=(1,),
        out_shape=[jax.ShapeDtypeStruct((cap, width), BF16)] * SIDE,
        in_specs=[
            pl.BlockSpec(memory_space=pltpu.SMEM),
            batch_of(rows.shape, batch),
            whole(gain.shape),
            whole(routing.shape),
            *[pl.BlockSpec((16, 128), lambda i: (0, 0)) for _ in after],
        ],
        out_specs=[whole((cap, width))] * SIDE,
        compiler_params=pltpu.CompilerParams(vmem_limit_bytes=12 << 20),
        name="pack",
    )(row, rows, gain, routing, *after)


def finish(raw, batch, batches, gate, onehot, back, span, earlier):
    toks, width = raw.shape[1:]
    cols = back[0].shape[1]

    def kernel(r, g, s, *rest):
        i, j = (lax.broadcasted_iota(jnp.int32, (toks, toks), d) for d in range(2))
        scale = jnp.sum(jnp.where(i == j, g[batch : batch + 1], 0.0), 1, keepdims=True)
        sums = sum(
            lax.dot_general(
                s[k], rest[k][...], (((0,), (0,)), ((), ())), preferred_element_type=F32
            )
            for k in range(SIDE)
        )
        rest[-1][0] = (r[0].astype(F32) + scale * sums).astype(BF16)

    return pl.pallas_call(
        kernel,
        grid=(1,),
        out_shape=jax.ShapeDtypeStruct((batches, toks, width), BF16),
        in_specs=[
            pl.BlockSpec((1, toks, cols), lambda i: (0, 0, span)),
            *[whole(v.shape) for v in (gate, onehot, *back)],
            *[pl.BlockSpec(memory_space=pl.ANY) for _ in earlier],
        ],
        out_specs=pl.BlockSpec((1, toks, cols), lambda i: (batch, 0, span)),
        input_output_aliases={3 + SIDE: 0} if earlier else {},
        compiler_params=pltpu.CompilerParams(vmem_limit_bytes=16 << 20),
        name="finish",
    )(raw, gate, onehot, *back, *earlier)


def per_device(acts, expert_ids, gates, norm_gain, w_gate_up, w_down):
    _, batches, toks, width = acts.shape
    cap = min(toks, 3 * toks // (2 * SIDE))
    row = lax.axis_index("et") // SIDE
    ids = expert_ids[0, :, :, 0]
    arriving = [shift_z(acts[0, b : b + 1], 1) for b in range(batches)]
    mine = []
    for b in range(batches):
        routing = ids[b : b + 1].astype(F32)
        packed = pack(arriving[b], 0, norm_gain, routing, row[None], cap, mine)
        landed = [packed[0]] + [shift_y(packed[k], k) for k in range(1, SIDE)]
        mine.append(jnp.concatenate(landed, 0))

    hidden = []
    for b in range(batches):
        rows = jnp.concatenate(gather_x(mine[b]), 0)
        both = jnp.einsum("rd,dkf->rkf", rows, w_gate_up[0, 0], preferred_element_type=F32)
        hidden.append((jax.nn.silu(both[:, 0]) * both[:, 1]).astype(BF16))

    for b in range(batches):
        part = jnp.dot(hidden[b], w_down[0, 0], preferred_element_type=F32).astype(BF16)
        part = part.reshape(SIDE, SIDE * cap, width)
        onehot = slot_map(ids[b], row, cap).reshape(SIDE, cap, toks)
        summed = scatter_sum_x([part[j] for j in range(SIDE)], BACK[b])
        total = summed[0].reshape(SIDE, cap, width)
        back = [total[0]] + [shift_y(total[k], -k) for k in range(1, SIDE)]
        if b == 0:
            out = finish(arriving[b], b, batches, gates[0], onehot, back, 0, [])
        else:
            from_slots = slot_map(ids[b], row, cap).T
            sums = jnp.dot(from_slots, jnp.concatenate(back, 0), preferred_element_type=F32)
            done = arriving[b].astype(F32) + gates[0, b][None, :, None] * sums[None]
            out = lax.dynamic_update_slice(out, done.astype(BF16), (b, 0, 0))
    return out[None]


def solution(mesh):
    in_specs = (
        P(("dp", "section"), None, "et", None),
        P(("dp", "section"), None, "et", None),
        P(("dp", "section"), None, "et"),
        P(("dp", "section"), None),
        P(("dp", "section"), "et", None, None, None),
        P(("dp", "section"), "et", None, None),
    )
    out_specs = P(("dp", "section"), None, "et", None)
    return jax.shard_map(
        per_device, mesh=mesh, in_specs=in_specs, out_specs=out_specs, check_vma=False
    )
```
